32 devices in a mesh: section: 4 (over x, core), win: 8 (over z, y).
Axes of the slice: x: 2, y: 2, z: 4, core: 2. Of those that a mesh axis runs over, the one named last changes fastest.
Arguments:
- latent: bfloat16 [24, 64, 256], P(None, 'win'), may hold values from -6 to 6
- anchors: int32 [16, 2], P('win'), may hold values from 0 to 56, as said below
- in_proj: bfloat16 [256, 1280], replicated, may hold values from -0.375 to 0.375
- pos_embed: bfloat16 [256, 1280], replicated, may hold values from -6 to 6
- section_w1: bfloat16 [4, 1280, 2560], P('section'), may hold values from -0.15625 to 0.15625
- section_w2: bfloat16 [4, 2560, 1280], P('section'), may hold values from -0.125 to 0.125
- section_gain: float32 [4, 1280], P('section'), may hold values from 0.5 to 1.5
- skip_w: bfloat16 [2560, 1280], replicated, may hold values from -0.125 to 0.125
- out_proj: bfloat16 [1280, 256], replicated, may hold values from -0.15625 to 0.15625
Outputs:
- noise_avg: bfloat16 [24, 64, 256], P('section', 'win')
The draws below stay inside these ranges and needn't reach their ends.
Inputs may be any that keep to these rules, and one draw needn't show every extreme that they name: Column 0 holds the row anchor, column 1 the column anchor; the windows are listed in an order drawn at random. Every column anchor that is a multiple of 8 below 64 appears in exactly 2 windows. Let g be a column anchor divided by 8. For even g, the row anchors of those windows are 0 and 8. For odd g, each row anchor lies anywhere from 0 to 8. Every token is covered by at least one window.
All inputs are finite; a program needn't handle non-finite values.
Results may differ from the reference program's by a relative error of at most 0.014.
Values may be sent and summed in bfloat16 or wider, within the bound.
A program may use at most 128 MiB of HBM per device.

```python
import jax
import jax.numpy as jnp
from jax import lax

D = 1280
HID = 2560
FEAT = 256
TILE = 16
STRIDE = 8
SECTIONS = 4
PW = 64
PH = 24
WINDOWS = 16


def draw_anchors(key, part):
    key = jax.random.fold_in(key, 11)
    order = jax.random.permutation(jax.random.fold_in(key, 1), WINDOWS)
    across = PW // STRIDE
    slot = order // across
    grid = order % across
    moved_row = jax.random.randint(jax.random.fold_in(key, 2), (WINDOWS,), 0, PH - TILE + 1)
    row_anchor = jnp.where(grid % 2 == 0, slot * STRIDE, moved_row)
    col_anchor = grid * STRIDE
    return jnp.stack([row_anchor, col_anchor], axis=1).astype(jnp.int32)


def block_levels(own_key, extent, split, low, top_value):
    level = 1.0
    for position, parts in split:
        draws = jax.random.uniform(jax.random.fold_in(jax.random.fold_in(own_key, 6), position), (parts,), jnp.float32, low / len(split), top_value / len(split))
        level = level * jnp.repeat(jnp.exp(draws), extent[position] // parts).reshape((-1,) + (1,) * (len(extent) - 1 - position))
    return level


def normal_values(rng, dims, deviation, limit, pieces=(), kind=jnp.bfloat16):
    values = jax.random.normal(rng, dims, jnp.float32) * deviation
    if len(pieces) > 0:
        values = block_levels(rng, dims, pieces, -0.22, 0.18) * values
    return jnp.clip(values, min=-limit, max=limit).astype(kind)


def setup_inputs(seed: int = 0) -> dict:
    key_of = jax.random.split(jax.random.key(seed), 10)
    latent = normal_values(key_of[0], (PH, PW, FEAT), 1.0, 6.0, ((1, 8),))
    anchors = draw_anchors(jax.random.fold_in(key_of[9], 71), 0)
    in_proj = normal_values(key_of[2], (FEAT, D), FEAT ** -0.5, 0.375)
    pos_embed = normal_values(key_of[3], (TILE * TILE, D), 1.0, 6.0)
    section_w1 = normal_values(key_of[4], (SECTIONS, D, HID), D ** -0.5, 0.15625, ((0, 4),))
    section_w2 = normal_values(key_of[5], (SECTIONS, HID, D), HID ** -0.5, 0.125, ((0, 4),))
    section_gain = jnp.clip(1.0 + 0.1 * jax.random.normal(key_of[6], (SECTIONS, D), jnp.float32), 0.5, 1.5)
    skip_w = normal_values(key_of[7], (2 * D, D), (2 * D) ** -0.5, 0.125)
    out_proj = normal_values(key_of[8], (D, FEAT), D ** -0.5, 0.15625)
    return {"latent": latent, "anchors": anchors, "in_proj": in_proj, "pos_embed": pos_embed, "section_w1": section_w1, "section_w2": section_w2, "section_gain": section_gain, "skip_w": skip_w, "out_proj": out_proj}


def rms_block(values, gain, w_first, w_second):
    factor = lax.rsqrt(lax.optimization_barrier(jnp.mean(values * values, axis=-1, keepdims=True)) + 1e-06)
    normed = (values * factor * gain).astype(jnp.bfloat16)
    hidden = jax.nn.gelu(jnp.dot(normed, w_first, preferred_element_type=jnp.float32), approximate=True).astype(jnp.bfloat16)
    return values + jnp.dot(hidden, w_second, preferred_element_type=jnp.float32)

def reference(latent, anchors, in_proj, pos_embed, section_w1, section_w2, section_gain, skip_w, out_proj):
    offsets = jnp.arange(TILE, dtype=jnp.int32)
    position_term = pos_embed.astype(jnp.float32)

    def one_window(anchor):
        row_index = anchor[0] + offsets
        col_index = (anchor[1] + offsets) % PW
        tiles = latent[row_index[:, None], col_index[None, :]].reshape(TILE * TILE, FEAT)
        embedded = jnp.dot(tiles, in_proj, preferred_element_type=jnp.float32) + position_term
        first = rms_block(embedded, section_gain[0], section_w1[0], section_w2[0]).astype(jnp.bfloat16)
        second = rms_block(first.astype(jnp.float32), section_gain[1], section_w1[1], section_w2[1]).astype(jnp.bfloat16)
        third = rms_block(second.astype(jnp.float32), section_gain[2], section_w1[2], section_w2[2]).astype(jnp.bfloat16)
        merged = jnp.dot(jnp.concatenate([third, first], axis=1), skip_w, preferred_element_type=jnp.float32)
        deep = rms_block(merged, section_gain[3], section_w1[3], section_w2[3]).astype(jnp.bfloat16)
        return jnp.dot(deep, out_proj, preferred_element_type=jnp.float32).astype(jnp.bfloat16)
    noises = lax.map(one_window, anchors)
    row_index = anchors[:, 0:1] + offsets[None, :]
    col_index = (anchors[:, 1:2] + offsets[None, :]) % PW
    placed = noises.reshape(WINDOWS, TILE, TILE, FEAT).astype(jnp.float32)
    totals = jnp.zeros((PH, PW, FEAT), jnp.float32).at[row_index[:, :, None], col_index[:, None, :]].add(placed)
    covered = jnp.zeros((PH, PW), jnp.float32).at[row_index[:, :, None], col_index[:, None, :]].add(1.0)
    return (totals / covered[..., None]).astype(jnp.bfloat16)
```

```python
import functools

import jax
import jax.numpy as jnp
from jax import lax
from jax.experimental import pallas as pl
from jax.experimental.pallas import tpu as pltpu
from jax.sharding import PartitionSpec as P

MESH = pl.DeviceIdType.MESH
TILE = 16
MB = 128
PIECES = 5


def gelu(x):
    return 0.5 * x * (1.0 + jnp.tanh(0.7978845608028654 * (x + 0.044715 * (x * x * x))))


def kernel(
    sections, slabs, height, width,
    latent, anchors, in_proj, pos_embed, w1_in, w2_in, gain_in, skip_in, out_in,
    result,
    panel, cast, marks, w1, w2, skip, proj, pos, outp, gain,
    received, skipped, produced, value, normed, sums, blocks, arrived,
    load_sem, mark_send, mark_recv, slab_send, slab_recv,
    next_send, next_recv, skip_send, skip_recv, done_send, done_recv,
):
    section = lax.axis_index("section")
    win = lax.axis_index("win")
    last = sections - 1
    count, rows = received.shape[0], received.shape[1]
    tokens = TILE * TILE
    half = height * width
    band = half // sections
    hidden = w1.shape[1]
    model = w1.shape[0]
    piece = hidden // PIECES
    after = lax.rem(win + 1, slabs)
    before = lax.rem(win + slabs - 1, slabs)

    def load(source, target, index):
        return pltpu.make_async_copy(source, target, load_sem.at[index])

    def w1_load(p):
        return load(w1_in.at[0, pl.ds(p * (model // PIECES), model // PIECES)],
                    w1.at[pl.ds(p * (model // PIECES), model // PIECES)], p)

    def w2_load(p):
        return load(w2_in.at[0, pl.ds(p * piece, piece)], w2.at[pl.ds(p * piece, piece)], PIECES + p)

    base = 2 * PIECES
    gain_load = load(gain_in, gain, base)
    proj_load = load(in_proj, proj, base + 1)
    pos_load = load(pos_embed, pos, base + 2)
    skip_load = load(skip_in, skip, base + 3)
    out_load = load(out_in, outp, base + 4)
    own_load = load(latent, panel.at[0], base + 5)

    barrier = pltpu.get_barrier_semaphore()

    def greet(to_section, to_win):
        pl.semaphore_signal(barrier, inc=1, device_id=(to_section, to_win), device_id_type=MESH)

    def greet_peer(step, carry):
        greet(section, lax.rem(win + step, slabs))
        return carry

    lax.fori_loop(1, slabs, greet_peer, 0)

    @pl.when(section > 0)
    def _():
        greet(section - 1, win)

    @pl.when(section == last)
    def _():
        greet(0, win)

    @pl.when(section < last)
    def _():
        greet(last, win)
        greet(last, before)

    @pl.when(section == 0)
    def _():
        own_load.start()
        proj_load.start()
        pos_load.start()

    gain_load.start()
    for p in range(PIECES):
        w1_load(p).start()
    for p in range(PIECES):
        w2_load(p).start()

    @pl.when(section == last)
    def _():
        skip_load.start()
        out_load.start()

    line = lax.broadcasted_iota(jnp.int32, (16, 128), 0)
    block = jnp.full((16, 128), -4096, jnp.int32)
    for i in range(anchors.shape[0]):
        block = jnp.where(line == i, anchors[i, 0], block)
        block = jnp.where(line == 8 + i, anchors[i, 1], block)
    marks[win] = block.astype(jnp.float32)

    @pl.when(section == 0)
    def _():
        pl.semaphore_wait(barrier, slabs - 1 + 2)

    @pl.when((section > 0) & (section < last))
    def _():
        pl.semaphore_wait(barrier, slabs - 1 + 1)

    @pl.when(section == last)
    def _():
        pl.semaphore_wait(barrier, slabs - 1 + 2 * last)

    def slab_copy():
        return pltpu.make_async_remote_copy(
            src_ref=latent, dst_ref=panel.at[1], send_sem=slab_send, recv_sem=slab_recv,
            device_id=(section, before), device_id_type=MESH)

    @pl.when(section == 0)
    def _():
        slab_copy().start()

    def mark_copy(step):
        return pltpu.make_async_remote_copy(
            src_ref=marks.at[win], dst_ref=marks.at[win],
            send_sem=mark_send.at[step], recv_sem=mark_recv.at[step],
            device_id=(section, lax.rem(win + step, slabs)), device_id_type=MESH)

    def mark_start(step, carry):
        mark_copy(step).start()
        return carry

    def mark_wait(step, carry):
        origin = lax.rem(win - step + slabs, slabs)
        pltpu.make_async_remote_copy(
            src_ref=marks.at[origin], dst_ref=marks.at[origin],
            send_sem=mark_send.at[step], recv_sem=mark_recv.at[step],
            device_id=(section, lax.rem(win + step, slabs)), device_id_type=MESH).wait_recv()
        return carry

    lax.fori_loop(1, slabs, mark_start, 0)
    lax.fori_loop(1, slabs, mark_wait, 0)

    def row_anchors(group):
        every = marks[...]
        row, col = every[:, 0:8, :], every[:, 8:16, :]
        match = col == (group * width).astype(jnp.float32)
        low = jnp.min(jnp.min(jnp.where(match, row, 4096.0), axis=0), axis=0, keepdims=True)
        high = jnp.max(jnp.max(jnp.where(match, row, -4096.0), axis=0), axis=0, keepdims=True)
        return low[:, 0:1], high[:, 0:1]

    low, high = row_anchors(win)

    def place(index, shape, dim):
        anchor = jnp.where(index < count // 2, low, high)
        inside = lax.rem(index, count // 2) * rows
        token = lax.broadcasted_iota(jnp.int32, shape, dim) + inside
        row, col = token // TILE, token % TILE
        fixed = (row * width + col % width + half * (col // width)).astype(jnp.float32)
        spot = lax.broadcasted_iota(jnp.int32, shape, 1 - dim).astype(jnp.float32)
        return (spot == fixed + anchor * float(width)).astype(jnp.bfloat16)

    def dot(a, b):
        return jnp.dot(a, b, preferred_element_type=jnp.float32)

    def rms_block():
        v = value[...]
        factor = lax.rsqrt(jnp.mean(v * v, axis=-1, keepdims=True) + 1e-06)
        normed[...] = (v * factor * gain[...]).astype(jnp.bfloat16)
        for p in range(PIECES):
            part = gelu(dot(normed[...], w1[:, p * piece:(p + 1) * piece])).astype(jnp.bfloat16)
            value[...] += dot(part, w2[p * piece:(p + 1) * piece, :])
        return value[...].astype(jnp.bfloat16)

    def next_copy(index, target):
        return pltpu.make_async_remote_copy(
            src_ref=produced.at[index], dst_ref=received.at[index],
            send_sem=next_send.at[index], recv_sem=next_recv.at[index],
            device_id=(target, win), device_id_type=MESH)

    def skip_copy(index):
        return pltpu.make_async_remote_copy(
            src_ref=produced.at[index], dst_ref=skipped.at[index],
            send_sem=skip_send.at[index], recv_sem=skip_recv.at[index],
            device_id=(last, win), device_id_type=MESH)

    def wait_weights():
        gain_load.wait()
        for p in range(PIECES):
            w1_load(p).wait()
        for p in range(PIECES):
            w2_load(p).wait()

    @pl.when(section == 0)
    def _():
        own_load.wait()
        proj_load.wait()
        pos_load.wait()
        slab_copy().wait_recv()
        both = jnp.concatenate([panel[0], panel[1]], axis=0)
        cast[...] = both
        wait_weights()

        def step(index, carry):
            tiles = dot(place(index, (rows, 2 * half), 0), cast[...]).astype(jnp.bfloat16)
            start = pl.multiple_of(lax.rem(index, count // 2) * rows, rows)
            value[...] = dot(tiles, proj[...]) + pos[pl.ds(start, rows), :].astype(jnp.float32)
            produced[index] = rms_block()
            next_copy(index, 1).start()
            skip_copy(index).start()
            return carry

        lax.fori_loop(0, count, step, 0)

        def drain(index, carry):
            next_copy(index, 1).wait_send()
            skip_copy(index).wait_send()
            return carry

        lax.fori_loop(0, count, drain, 0)
        slab_copy().wait_send()

    @pl.when((section > 0) & (section < last))
    def _():
        wait_weights()

        def step(index, carry):
            next_copy(index, section + 1).wait_recv()
            value[...] = received[index].astype(jnp.float32)
            produced[index] = rms_block()
            next_copy(index, section + 1).start()
            return carry

        lax.fori_loop(0, count, step, 0)

        def drain(index, carry):
            next_copy(index, section + 1).wait_send()
            return carry

        lax.fori_loop(0, count, drain, 0)

    def done_copy(target, side):
        return pltpu.make_async_remote_copy(
            src_ref=blocks.at[pl.ds(pl.multiple_of((side * sections + target) * band, 16), band)],
            dst_ref=arrived.at[side],
            send_sem=done_send.at[side, target], recv_sem=done_recv.at[side],
            device_id=(target, after if side else win), device_id_type=MESH)

    @pl.when(section == last)
    def _():
        wait_weights()
        skip_load.wait()
        out_load.wait()
        sums[...] = jnp.zeros_like(sums)

        def step(index, carry):
            next_copy(index, 0).wait_recv()
            skip_copy(index).wait_recv()
            value[...] = dot(received[index], skip[:model, :]) + dot(skipped[index], skip[model:, :])
            noise = dot(rms_block(), outp[...]).astype(jnp.bfloat16)
            sums[...] += dot(place(index, (2 * half, rows), 1), noise)
            return carry

        lax.fori_loop(0, count, step, 0)
        blocks[...] = sums[...].astype(jnp.bfloat16)
        for target in range(sections):
            done_copy(target, 1).start()
        for target in range(sections - 1):
            done_copy(target, 0).start()
        arrived[0] = blocks[pl.ds(last * band, band), :]

    lowest, highest = row_anchors(before)
    line = lax.broadcasted_iota(jnp.int32, (band, 128), 0) // width + section * (height // sections)
    line = line.astype(jnp.float32)
    covered = jnp.zeros((band, 128), jnp.float32)
    for anchor in (low, high, lowest, highest):
        covered += jnp.where((line >= anchor) & (line < anchor + float(TILE)), 1.0, 0.0)

    @pl.when(section < last)
    def _():
        done_copy(0, 0).wait_recv()

    done_copy(0, 1).wait_recv()
    total = arrived[0].astype(jnp.float32) + arrived[1].astype(jnp.float32)
    result[...] = (total / covered[:, 0:1]).astype(jnp.bfloat16)

    @pl.when(section == last)
    def _():
        for target in range(sections):
            done_copy(target, 1).wait_send()
        for target in range(sections - 1):
            done_copy(target, 0).wait_send()

    def mark_drain(step, carry):
        mark_copy(step).wait_send()
        return carry

    lax.fori_loop(1, slabs, mark_drain, 0)


def solution(mesh):
    sections, slabs = mesh.shape["section"], mesh.shape["win"]

    def per_device(latent, anchors, in_proj, pos_embed, w1, w2, gain, skip_w, out_proj):
        height, width, feat = latent.shape
        model, hidden = w1.shape[1:]
        half = height * width
        band = half // sections
        rows = MB
        count = anchors.shape[0] * TILE * TILE // rows
        bf16, f32 = jnp.bfloat16, jnp.float32
        hbm = pl.BlockSpec(memory_space=pl.ANY)
        dma = pltpu.SemaphoreType.DMA
        out = pl.pallas_call(
            functools.partial(kernel, sections, slabs, height, width),
            out_shape=jax.ShapeDtypeStruct((band, feat), bf16),
            in_specs=[hbm, pl.BlockSpec(memory_space=pltpu.SMEM)] + [hbm] * 7,
            out_specs=pl.BlockSpec(memory_space=pltpu.VMEM),
            scratch_shapes=[
                pltpu.VMEM((2, half, feat), bf16),
                pltpu.VMEM((2 * half, feat), bf16),
                pltpu.VMEM((slabs, 16, 128), f32),
                pltpu.VMEM((model, hidden), bf16),
                pltpu.VMEM((hidden, model), bf16),
                pltpu.VMEM((2 * model, model), bf16),
                pltpu.VMEM((feat, model), bf16),
                pltpu.VMEM((TILE * TILE, model), bf16),
                pltpu.VMEM((model, feat), bf16),
                pltpu.VMEM((1, model), f32),
                pltpu.VMEM((count, rows, model), bf16),
                pltpu.VMEM((count, rows, model), bf16),
                pltpu.VMEM((count, rows, model), bf16),
                pltpu.VMEM((rows, model), f32),
                pltpu.VMEM((rows, model), bf16),
                pltpu.VMEM((2 * half, feat), f32),
                pltpu.VMEM((2 * half, feat), bf16),
                pltpu.VMEM((2, band, feat), bf16),
                dma((2 * PIECES + 6,)),
                dma((slabs,)),
                dma((slabs,)),
                dma,
                dma,
                dma((count,)),
                dma((count,)),
                dma((count,)),
                dma((count,)),
                dma((2, sections)),
                dma((2,)),
            ],
            compiler_params=pltpu.CompilerParams(
                collective_id=0, has_side_effects=True, vmem_limit_bytes=56 * 1024 * 1024),
        )(latent.reshape(half, feat), anchors, in_proj, pos_embed, w1, w2, gain, skip_w, out_proj)
        return out.reshape(height // sections, width, feat)

    return jax.shard_map(
        per_device,
        mesh=mesh,
        in_specs=(
            P(None, "win", None), P("win", None), P(), P(), P("section", None, None),
            P("section", None, None), P("section", None), P(), P(),
        ),
        out_specs=P("section", "win", None),
        check_vma=False,
    )
```

```python
import functools

import jax
import jax.numpy as jnp
from jax import lax
from jax.experimental import pallas as pl
from jax.experimental.pallas import tpu as pltpu
from jax.sharding import PartitionSpec as P

MESH = pl.DeviceIdType.MESH
TILE = 16
MB = 128
PIECES = 5


def gelu(x):
    return 0.5 * x * (1.0 + jnp.tanh(0.7978845608028654 * (x + 0.044715 * (x * x * x))))


def kernel(
    sections, slabs, height, width,
    latent, anchors, in_proj, pos_embed, w1_in, w2_in, gain_in, skip_in, out_in,
    result,
    panel, cast, marks, w1, w2, skip, proj, pos, outp, gain,
    received, skipped, produced, value, normed, sums, blocks, arrived,
    load_sem, mark_send, mark_recv, slab_send, slab_recv,
    next_send, next_recv, skip_send, skip_recv, done_send, done_recv, credit,
):
    section = lax.axis_index("section")
    win = lax.axis_index("win")
    last = sections - 1
    count, rows = received.shape[0], received.shape[1]
    tokens = TILE * TILE
    half = height * width
    band = half // sections
    hidden = w1.shape[1]
    model = w1.shape[0]
    piece = hidden // PIECES
    after = lax.rem(win + 1, slabs)
    before = lax.rem(win + slabs - 1, slabs)

    def load(source, target, index):
        return pltpu.make_async_copy(source, target, load_sem.at[index])

    def w1_load(p):
        return load(w1_in.at[0, pl.ds(p * (model // PIECES), model // PIECES)],
                    w1.at[pl.ds(p * (model // PIECES), model // PIECES)], p)

    def w2_load(p):
        return load(w2_in.at[0, pl.ds(p * piece, piece)], w2.at[pl.ds(p * piece, piece)], PIECES + p)

    base = 2 * PIECES
    gain_load = load(gain_in, gain, base)
    proj_load = load(in_proj, proj, base + 1)
    pos_load = load(pos_embed, pos, base + 2)
    skip_load = load(skip_in, skip, base + 3)
    out_load = load(out_in, outp, base + 4)
    own_load = load(latent, panel.at[0], base + 5)

    barrier = pltpu.get_barrier_semaphore()

    def greet(to_section, to_win):
        pl.semaphore_signal(barrier, inc=1, device_id=(to_section, to_win), device_id_type=MESH)

    def greet_peer(step, carry):
        greet(section, lax.rem(win + step, slabs))
        return carry

    lax.fori_loop(1, slabs, greet_peer, 0)

    @pl.when(section > 0)
    def _():
        greet(section - 1, win)

    @pl.when(section == last)
    def _():
        greet(0, win)

    @pl.when(section == 0)
    def _():
        greet(1, win)

    @pl.when(section < last)
    def _():
        greet(last, win)
        greet(last, before)

    @pl.when(section == 0)
    def _():
        own_load.start()
        proj_load.start()
        pos_load.start()

    gain_load.start()
    for p in range(PIECES):
        w1_load(p).start()
    for p in range(PIECES):
        w2_load(p).start()

    @pl.when(section == last)
    def _():
        skip_load.start()
        out_load.start()

    line = lax.broadcasted_iota(jnp.int32, (16, 128), 0)
    block = jnp.full((16, 128), -4096, jnp.int32)
    for i in range(anchors.shape[0]):
        block = jnp.where(line == i, anchors[i, 0], block)
        block = jnp.where(line == 8 + i, anchors[i, 1], block)
    marks[win] = block.astype(jnp.float32)

    @pl.when(section == 0)
    def _():
        pl.semaphore_wait(barrier, slabs - 1 + 2)

    @pl.when(section == 1)
    def _():
        pl.semaphore_wait(barrier, slabs - 1 + 2)

    @pl.when((section > 1) & (section < last))
    def _():
        pl.semaphore_wait(barrier, slabs - 1 + 1)

    @pl.when(section == last)
    def _():
        pl.semaphore_wait(barrier, slabs - 1 + 2 * last)

    def slab_copy():
        return pltpu.make_async_remote_copy(
            src_ref=latent, dst_ref=panel.at[1], send_sem=slab_send, recv_sem=slab_recv,
            device_id=(section, before), device_id_type=MESH)

    @pl.when(section == 0)
    def _():
        slab_copy().start()

    def mark_copy(step):
        return pltpu.make_async_remote_copy(
            src_ref=marks.at[win], dst_ref=marks.at[win],
            send_sem=mark_send.at[step], recv_sem=mark_recv.at[step],
            device_id=(section, lax.rem(win + step, slabs)), device_id_type=MESH)

    def mark_start(step, carry):
        mark_copy(step).start()
        return carry

    def mark_wait(step, carry):
        origin = lax.rem(win - step + slabs, slabs)
        pltpu.make_async_remote_copy(
            src_ref=marks.at[origin], dst_ref=marks.at[origin],
            send_sem=mark_send.at[step], recv_sem=mark_recv.at[step],
            device_id=(section, lax.rem(win + step, slabs)), device_id_type=MESH).wait_recv()
        return carry

    lax.fori_loop(1, slabs, mark_start, 0)
    lax.fori_loop(1, slabs, mark_wait, 0)

    def row_anchors(group):
        every = marks[...]
        row, col = every[:, 0:8, :], every[:, 8:16, :]
        match = col == (group * width).astype(jnp.float32)
        low = jnp.min(jnp.min(jnp.where(match, row, 4096.0), axis=0), axis=0, keepdims=True)
        high = jnp.max(jnp.max(jnp.where(match, row, -4096.0), axis=0), axis=0, keepdims=True)
        return low[:, 0:1], high[:, 0:1]

    low, high = row_anchors(win)

    def place(index, shape, dim):
        anchor = jnp.where(index < count // 2, low, high)
        inside = lax.rem(index, count // 2) * rows
        token = lax.broadcasted_iota(jnp.int32, shape, dim) + inside
        row, col = token // TILE, token % TILE
        fixed = (row * width + col % width + half * (col // width)).astype(jnp.float32)
        spot = lax.broadcasted_iota(jnp.int32, shape, 1 - dim).astype(jnp.float32)
        return (spot == fixed + anchor * float(width)).astype(jnp.bfloat16)

    def dot(a, b):
        return jnp.dot(a, b, preferred_element_type=jnp.float32)

    def rms_block():
        v = value[...]
        factor = lax.rsqrt(jnp.mean(v * v, axis=-1, keepdims=True) + 1e-06)
        normed[...] = (v * factor * gain[...]).astype(jnp.bfloat16)
        for p in range(PIECES):
            part = gelu(dot(normed[...], w1[:, p * piece:(p + 1) * piece])).astype(jnp.bfloat16)
            value[...] += dot(part, w2[p * piece:(p + 1) * piece, :])
        return value[...].astype(jnp.bfloat16)

    def next_copy(index, target):
        return pltpu.make_async_remote_copy(
            src_ref=produced.at[index], dst_ref=received.at[index],
            send_sem=next_send.at[index], recv_sem=next_recv.at[index],
            device_id=(target, win), device_id_type=MESH)

    def skip_copy(index):
        return pltpu.make_async_remote_copy(
            src_ref=produced.at[index], dst_ref=skipped.at[index],
            send_sem=skip_send.at[index], recv_sem=skip_recv.at[index],
            device_id=(last, win), device_id_type=MESH)

    def wait_weights():
        gain_load.wait()
        for p in range(PIECES):
            w1_load(p).wait()
        for p in range(PIECES):
            w2_load(p).wait()

    @pl.when(section == 0)
    def _():
        own_load.wait()
        proj_load.wait()
        pos_load.wait()
        slab_copy().wait_recv()
        both = jnp.concatenate([panel[0], panel[1]], axis=0)
        cast[...] = both
        wait_weights()

        def step(index, carry):
            tiles = dot(place(index, (rows, 2 * half), 0), cast[...]).astype(jnp.bfloat16)
            start = pl.multiple_of(lax.rem(index, count // 2) * rows, rows)
            value[...] = dot(tiles, proj[...]) + pos[pl.ds(start, rows), :].astype(jnp.float32)
            produced[index] = rms_block()
            next_copy(index, 1).start()

            @pl.when(index == 0)
            def _():
                skip_copy(index).start()

            return carry

        lax.fori_loop(0, count, step, 0)
        for index in range(1, count):
            pl.semaphore_wait(credit, 1 if index < count - 1 else 2)
            skip_copy(index).start()

        def drain(index, carry):
            next_copy(index, 1).wait_send()
            skip_copy(index).wait_send()
            return carry

        lax.fori_loop(0, count, drain, 0)
        slab_copy().wait_send()

    @pl.when((section > 0) & (section < last))
    def _():
        wait_weights()

        def step(index, carry):
            next_copy(index, section + 1).wait_recv()
            value[...] = received[index].astype(jnp.float32)
            produced[index] = rms_block()
            next_copy(index, section + 1).start()

            @pl.when(index > 0)
            def _():
                left(index - 1)

            return carry

        def left(index):
            next_copy(index, section + 1).wait_send()

            @pl.when(section == 1)
            def _():
                pl.semaphore_signal(credit, inc=1, device_id=(0, win), device_id_type=MESH)

        lax.fori_loop(0, count, step, 0)
        left(count - 1)

    def done_copy(target, side):
        return pltpu.make_async_remote_copy(
            src_ref=blocks.at[pl.ds(pl.multiple_of((side * sections + target) * band, 16), band)],
            dst_ref=arrived.at[side],
            send_sem=done_send.at[side, target], recv_sem=done_recv.at[side],
            device_id=(target, after if side else win), device_id_type=MESH)

    @pl.when(section == last)
    def _():
        wait_weights()
        skip_load.wait()
        out_load.wait()
        sums[...] = jnp.zeros_like(sums)

        def step(index, carry):
            next_copy(index, 0).wait_recv()
            value[...] = dot(received[index], skip[:model, :])
            skip_copy(index).wait_recv()
            value[...] += dot(skipped[index], skip[model:, :])
            noise = dot(rms_block(), outp[...]).astype(jnp.bfloat16)
            sums[...] += dot(place(index, (2 * half, rows), 1), noise)
            return carry

        lax.fori_loop(0, count, step, 0)
        blocks[...] = sums[...].astype(jnp.bfloat16)
        for target in range(sections):
            done_copy(target, 1).start()
        for target in range(sections - 1):
            done_copy(target, 0).start()
        arrived[0] = blocks[pl.ds(last * band, band), :]

    lowest, highest = row_anchors(before)
    line = lax.broadcasted_iota(jnp.int32, (band, 128), 0) // width + section * (height // sections)
    line = line.astype(jnp.float32)
    covered = jnp.zeros((band, 128), jnp.float32)
    for anchor in (low, high, lowest, highest):
        covered += jnp.where((line >= anchor) & (line < anchor + float(TILE)), 1.0, 0.0)

    @pl.when(section < last)
    def _():
        done_copy(0, 0).wait_recv()

    done_copy(0, 1).wait_recv()
    total = arrived[0].astype(jnp.float32) + arrived[1].astype(jnp.float32)
    result[...] = (total / covered[:, 0:1]).astype(jnp.bfloat16)

    @pl.when(section == last)
    def _():
        for target in range(sections):
            done_copy(target, 1).wait_send()
        for target in range(sections - 1):
            done_copy(target, 0).wait_send()

    def mark_drain(step, carry):
        mark_copy(step).wait_send()
        return carry

    lax.fori_loop(1, slabs, mark_drain, 0)


def solution(mesh):
    sections, slabs = mesh.shape["section"], mesh.shape["win"]

    def per_device(latent, anchors, in_proj, pos_embed, w1, w2, gain, skip_w, out_proj):
        height, width, feat = latent.shape
        model, hidden = w1.shape[1:]
        half = height * width
        band = half // sections
        rows = MB
        count = anchors.shape[0] * TILE * TILE // rows
        bf16, f32 = jnp.bfloat16, jnp.float32
        hbm = pl.BlockSpec(memory_space=pl.ANY)
        dma = pltpu.SemaphoreType.DMA
        out = pl.pallas_call(
            functools.partial(kernel, sections, slabs, height, width),
            out_shape=jax.ShapeDtypeStruct((band, feat), bf16),
            in_specs=[hbm, pl.BlockSpec(memory_space=pltpu.SMEM)] + [hbm] * 7,
            out_specs=pl.BlockSpec(memory_space=pltpu.VMEM),
            scratch_shapes=[
                pltpu.VMEM((2, half, feat), bf16),
                pltpu.VMEM((2 * half, feat), bf16),
                pltpu.VMEM((slabs, 16, 128), f32),
                pltpu.VMEM((model, hidden), bf16),
                pltpu.VMEM((hidden, model), bf16),
                pltpu.VMEM((2 * model, model), bf16),
                pltpu.VMEM((feat, model), bf16),
                pltpu.VMEM((TILE * TILE, model), bf16),
                pltpu.VMEM((model, feat), bf16),
                pltpu.VMEM((1, model), f32),
                pltpu.VMEM((count, rows, model), bf16),
                pltpu.VMEM((count, rows, model), bf16),
                pltpu.VMEM((count, rows, model), bf16),
                pltpu.VMEM((rows, model), f32),
                pltpu.VMEM((rows, model), bf16),
                pltpu.VMEM((2 * half, feat), f32),
                pltpu.VMEM((2 * half, feat), bf16),
                pltpu.VMEM((2, band, feat), bf16),
                dma((2 * PIECES + 6,)),
                dma((slabs,)),
                dma((slabs,)),
                dma,
                dma,
                dma((count,)),
                dma((count,)),
                dma((count,)),
                dma((count,)),
                dma((2, sections)),
                dma((2,)),
                pltpu.SemaphoreType.REGULAR,
            ],
            compiler_params=pltpu.CompilerParams(
                collective_id=0, has_side_effects=True, vmem_limit_bytes=56 * 1024 * 1024),
        )(latent.reshape(half, feat), anchors, in_proj, pos_embed, w1, w2, gain, skip_w, out_proj)
        return out.reshape(height // sections, width, feat)

    return jax.shard_map(
        per_device,
        mesh=mesh,
        in_specs=(
            P(None, "win", None), P("win", None), P(), P(), P("section", None, None),
            P("section", None, None), P("section", None), P(), P(),
        ),
        out_specs=P("section", "win", None),
        check_vma=False,
    )
```

```python
import functools

import jax
import jax.numpy as jnp
from jax import lax
from jax.experimental import pallas as pl
from jax.experimental.pallas import tpu as pltpu
from jax.sharding import PartitionSpec as P

MESH = pl.DeviceIdType.MESH
TILE = 16
MB = 128
PIECES = 5
PARTS = 5


def gelu(x):
    return 0.5 * x * (1.0 + jnp.tanh(0.7978845608028654 * (x + 0.044715 * (x * x * x))))


def kernel(
    sections, slabs, height, width,
    latent, anchors, in_proj, pos_embed, w1_in, w2_in, gain_in, skip_in, out_in,
    result,
    panel, cast, marks, w1, w2, skip, proj, pos, outp, gain,
    received, skipped, produced, value, normed, units, sums, blocks, arrived,
    load_sem, mark_send, mark_recv, slab_send, slab_recv,
    next_send, next_recv, skip_send, skip_recv, done_send, done_recv, credit,
):
    section = lax.axis_index("section")
    win = lax.axis_index("win")
    last = sections - 1
    count, rows = received.shape[0], received.shape[2]
    wide = received.shape[3]
    tokens = TILE * TILE
    half = height * width
    band = half // sections
    hidden = w1.shape[1]
    model = w1.shape[0]
    piece = hidden // PIECES
    after = lax.rem(win + 1, slabs)
    before = lax.rem(win + slabs - 1, slabs)

    def load(source, target, index):
        return pltpu.make_async_copy(source, target, load_sem.at[index])

    def w1_load(p):
        return load(w1_in.at[0, pl.ds(p * (model // PIECES), model // PIECES)],
                    w1.at[pl.ds(p * (model // PIECES), model // PIECES)], p)

    def w2_load(p):
        return load(w2_in.at[0, pl.ds(p * piece, piece)], w2.at[pl.ds(p * piece, piece)], PIECES + p)

    base = 2 * PIECES
    gain_load = load(gain_in, gain, base)
    proj_load = load(in_proj, proj, base + 1)
    pos_load = load(pos_embed, pos, base + 2)
    skip_load = load(skip_in, skip, base + 3)
    out_load = load(out_in, outp, base + 4)
    own_load = load(latent, panel.at[0], base + 5)

    barrier = pltpu.get_barrier_semaphore()

    def greet(to_section, to_win):
        pl.semaphore_signal(barrier, inc=1, device_id=(to_section, to_win), device_id_type=MESH)

    def greet_peer(step, carry):
        greet(section, lax.rem(win + step, slabs))
        return carry

    lax.fori_loop(1, slabs, greet_peer, 0)

    @pl.when(section > 0)
    def _():
        greet(section - 1, win)

    @pl.when(section == last)
    def _():
        greet(0, win)

    @pl.when(section == 0)
    def _():
        greet(1, win)

    @pl.when(section < last)
    def _():
        greet(last, win)
        greet(last, before)

    @pl.when(section == 0)
    def _():
        own_load.start()
        proj_load.start()
        pos_load.start()

    gain_load.start()
    for p in range(PIECES):
        w1_load(p).start()
    for p in range(PIECES):
        w2_load(p).start()

    @pl.when(section == last)
    def _():
        skip_load.start()
        out_load.start()

    line = lax.broadcasted_iota(jnp.int32, (16, 128), 0)
    block = jnp.full((16, 128), -4096, jnp.int32)
    for i in range(anchors.shape[0]):
        block = jnp.where(line == i, anchors[i, 0], block)
        block = jnp.where(line == 8 + i, anchors[i, 1], block)
    marks[win] = block.astype(jnp.float32)

    @pl.when(section == 0)
    def _():
        pl.semaphore_wait(barrier, slabs - 1 + 2)

    @pl.when(section == 1)
    def _():
        pl.semaphore_wait(barrier, slabs - 1 + 2)

    @pl.when((section > 1) & (section < last))
    def _():
        pl.semaphore_wait(barrier, slabs - 1 + 1)

    @pl.when(section == last)
    def _():
        pl.semaphore_wait(barrier, slabs - 1 + 2 * last)

    def slab_copy():
        return pltpu.make_async_remote_copy(
            src_ref=latent, dst_ref=panel.at[1], send_sem=slab_send, recv_sem=slab_recv,
            device_id=(section, before), device_id_type=MESH)

    @pl.when(section == 0)
    def _():
        slab_copy().start()

    def mark_copy(step):
        return pltpu.make_async_remote_copy(
            src_ref=marks.at[win], dst_ref=marks.at[win],
            send_sem=mark_send.at[step], recv_sem=mark_recv.at[step],
            device_id=(section, lax.rem(win + step, slabs)), device_id_type=MESH)

    def mark_start(step, carry):
        mark_copy(step).start()
        return carry

    def mark_wait(step, carry):
        origin = lax.rem(win - step + slabs, slabs)
        pltpu.make_async_remote_copy(
            src_ref=marks.at[origin], dst_ref=marks.at[origin],
            send_sem=mark_send.at[step], recv_sem=mark_recv.at[step],
            device_id=(section, lax.rem(win + step, slabs)), device_id_type=MESH).wait_recv()
        return carry

    lax.fori_loop(1, slabs, mark_start, 0)
    lax.fori_loop(1, slabs, mark_wait, 0)

    def row_anchors(group):
        every = marks[...]
        row, col = every[:, 0:8, :], every[:, 8:16, :]
        match = col == (group * width).astype(jnp.float32)
        low = jnp.min(jnp.min(jnp.where(match, row, 4096.0), axis=0), axis=0, keepdims=True)
        high = jnp.max(jnp.max(jnp.where(match, row, -4096.0), axis=0), axis=0, keepdims=True)
        return low[:, 0:1], high[:, 0:1]

    low, high = row_anchors(win)

    def place(index, shape, dim):
        anchor = jnp.where(index < count // 2, low, high)
        inside = lax.rem(index, count // 2) * rows
        token = lax.broadcasted_iota(jnp.int32, shape, dim) + inside
        row, col = token // TILE, token % TILE
        fixed = (row * width + col % width + half * (col // width)).astype(jnp.float32)
        spot = lax.broadcasted_iota(jnp.int32, shape, 1 - dim).astype(jnp.float32)
        return (spot == fixed + anchor * float(width)).astype(jnp.bfloat16)

    def dot(a, b):
        return jnp.dot(a, b, preferred_element_type=jnp.float32)

    def joined(ref, index):
        return jnp.concatenate([ref[index, p] for p in range(PARTS)], axis=1)

    def rms_block(emit, between=None):
        v = value[...]
        factor = lax.rsqrt(jnp.mean(v * v, axis=-1, keepdims=True) + 1e-06)
        normed[...] = (v * factor * gain[...]).astype(jnp.bfloat16)
        for p in range(PIECES):
            part = gelu(dot(normed[...], w1[:, p * piece:(p + 1) * piece]))
            units[:, p * piece:(p + 1) * piece] = part.astype(jnp.bfloat16)
        if between is not None:
            between()
        for p in range(PARTS):
            here = slice(p * wide, (p + 1) * wide)
            emit(p, (value[:, here] + dot(units[...], w2[:, here])).astype(jnp.bfloat16))

    def cut(ref, index, p):
        return ref.at[index] if p is None else ref.at[index, p]

    def next_copy(index, target, p=None):
        return pltpu.make_async_remote_copy(
            src_ref=cut(produced, index, p), dst_ref=cut(received, index, p),
            send_sem=next_send.at[index], recv_sem=next_recv.at[index],
            device_id=(target, win), device_id_type=MESH)

    def skip_copy(index, p=None):
        return pltpu.make_async_remote_copy(
            src_ref=cut(produced, index, p), dst_ref=cut(skipped, index, p),
            send_sem=skip_send.at[index], recv_sem=skip_recv.at[index],
            device_id=(last, win), device_id_type=MESH)

    def wait_first():
        gain_load.wait()
        for p in range(PIECES):
            w1_load(p).wait()

    def wait_second():
        for p in range(PIECES):
            w2_load(p).wait()

    def wait_weights():
        wait_first()
        wait_second()

    @pl.when(section == 0)
    def _():
        own_load.wait()
        proj_load.wait()
        pos_load.wait()
        slab_copy().wait_recv()
        both = jnp.concatenate([panel[0], panel[1]], axis=0)
        cast[...] = both
        wait_first()

        def step(index, carry):
            tiles = dot(place(index, (rows, 2 * half), 0), cast[...]).astype(jnp.bfloat16)
            start = pl.multiple_of(lax.rem(index, count // 2) * rows, rows)
            value[...] = dot(tiles, proj[...]) + pos[pl.ds(start, rows), :].astype(jnp.float32)

            def emit(p, part):
                produced[index, p] = part
                next_copy(index, 1, p).start()

            rms_block(emit, lambda: pl.when(index == 0)(wait_second))

            @pl.when(index == 0)
            def _():
                for p in range(PARTS):
                    skip_copy(index, p).start()

            return carry

        lax.fori_loop(0, count, step, 0)
        for index in range(1, count):
            pl.semaphore_wait(credit, 1 if index < count - 1 else 2)
            for p in range(PARTS):
                skip_copy(index, p).start()

        def drain(index, carry):
            next_copy(index, 1).wait_send()
            skip_copy(index).wait_send()
            return carry

        lax.fori_loop(0, count, drain, 0)
        slab_copy().wait_send()

    @pl.when((section > 0) & (section < last))
    def _():
        wait_weights()

        def step(index, carry):
            next_copy(index, section + 1).wait_recv()
            value[...] = joined(received, index).astype(jnp.float32)

            def emit(p, part):
                produced[index, p] = part
                next_copy(index, section + 1, p).start()

            rms_block(emit)

            @pl.when(index > 0)
            def _():
                left(index - 1)

            return carry

        def left(index):
            next_copy(index, section + 1).wait_send()

            @pl.when(section == 1)
            def _():
                pl.semaphore_signal(credit, inc=1, device_id=(0, win), device_id_type=MESH)

        lax.fori_loop(0, count, step, 0)
        left(count - 1)

    def done_copy(target, side):
        return pltpu.make_async_remote_copy(
            src_ref=blocks.at[pl.ds(pl.multiple_of((side * sections + target) * band, 16), band)],
            dst_ref=arrived.at[side],
            send_sem=done_send.at[side, target], recv_sem=done_recv.at[side],
            device_id=(target, after if side else win), device_id_type=MESH)

    @pl.when(section == last)
    def _():
        wait_weights()
        skip_load.wait()
        out_load.wait()
        sums[...] = jnp.zeros_like(sums)

        def step(index, carry):
            next_copy(index, 0).wait_recv()
            value[...] = dot(joined(received, index), skip[:model, :])
            skip_copy(index).wait_recv()
            value[...] += dot(joined(skipped, index), skip[model:, :])

            def emit(p, part):
                normed[:, p * wide:(p + 1) * wide] = part

            rms_block(emit)
            noise = dot(normed[...], outp[...]).astype(jnp.bfloat16)
            sums[...] += dot(place(index, (2 * half, rows), 1), noise)
            return carry

        lax.fori_loop(0, count, step, 0)
        blocks[...] = sums[...].astype(jnp.bfloat16)
        for target in range(sections):
            done_copy(target, 1).start()
        for target in range(sections - 1):
            done_copy(target, 0).start()
        arrived[0] = blocks[pl.ds(last * band, band), :]

    lowest, highest = row_anchors(before)
    line = lax.broadcasted_iota(jnp.int32, (band, 128), 0) // width + section * (height // sections)
    line = line.astype(jnp.float32)
    covered = jnp.zeros((band, 128), jnp.float32)
    for anchor in (low, high, lowest, highest):
        covered += jnp.where((line >= anchor) & (line < anchor + float(TILE)), 1.0, 0.0)

    @pl.when(section < last)
    def _():
        done_copy(0, 0).wait_recv()

    done_copy(0, 1).wait_recv()
    total = arrived[0].astype(jnp.float32) + arrived[1].astype(jnp.float32)
    result[...] = (total / covered[:, 0:1]).astype(jnp.bfloat16)

    @pl.when(section == last)
    def _():
        for target in range(sections):
            done_copy(target, 1).wait_send()
        for target in range(sections - 1):
            done_copy(target, 0).wait_send()

    def mark_drain(step, carry):
        mark_copy(step).wait_send()
        return carry

    lax.fori_loop(1, slabs, mark_drain, 0)


def solution(mesh):
    sections, slabs = mesh.shape["section"], mesh.shape["win"]

    def per_device(latent, anchors, in_proj, pos_embed, w1, w2, gain, skip_w, out_proj):
        height, width, feat = latent.shape
        model, hidden = w1.shape[1:]
        half = height * width
        band = half // sections
        rows = MB
        count = anchors.shape[0] * TILE * TILE // rows
        bf16, f32 = jnp.bfloat16, jnp.float32
        hbm = pl.BlockSpec(memory_space=pl.ANY)
        dma = pltpu.SemaphoreType.DMA
        out = pl.pallas_call(
            functools.partial(kernel, sections, slabs, height, width),
            out_shape=jax.ShapeDtypeStruct((band, feat), bf16),
            in_specs=[hbm, pl.BlockSpec(memory_space=pltpu.SMEM)] + [hbm] * 7,
            out_specs=pl.BlockSpec(memory_space=pltpu.VMEM),
            scratch_shapes=[
                pltpu.VMEM((2, half, feat), bf16),
                pltpu.VMEM((2 * half, feat), bf16),
                pltpu.VMEM((slabs, 16, 128), f32),
                pltpu.VMEM((model, hidden), bf16),
                pltpu.VMEM((hidden, model), bf16),
                pltpu.VMEM((2 * model, model), bf16),
                pltpu.VMEM((feat, model), bf16),
                pltpu.VMEM((TILE * TILE, model), bf16),
                pltpu.VMEM((model, feat), bf16),
                pltpu.VMEM((1, model), f32),
                pltpu.VMEM((count, PARTS, rows, model // PARTS), bf16),
                pltpu.VMEM((count, PARTS, rows, model // PARTS), bf16),
                pltpu.VMEM((count, PARTS, rows, model // PARTS), bf16),
                pltpu.VMEM((rows, model), f32),
                pltpu.VMEM((rows, model), bf16),
                pltpu.VMEM((rows, hidden), bf16),
                pltpu.VMEM((2 * half, feat), f32),
                pltpu.VMEM((2 * half, feat), bf16),
                pltpu.VMEM((2, band, feat), bf16),
                dma((2 * PIECES + 6,)),
                dma((slabs,)),
                dma((slabs,)),
                dma,
                dma,
                dma((count,)),
                dma((count,)),
                dma((count,)),
                dma((count,)),
                dma((2, sections)),
                dma((2,)),
                pltpu.SemaphoreType.REGULAR,
            ],
            compiler_params=pltpu.CompilerParams(
                collective_id=0, has_side_effects=True, vmem_limit_bytes=56 * 1024 * 1024),
        )(latent.reshape(half, feat), anchors, in_proj, pos_embed, w1, w2, gain, skip_w, out_proj)
        return out.reshape(height // sections, width, feat)

    return jax.shard_map(
        per_device,
        mesh=mesh,
        in_specs=(
            P(None, "win", None), P("win", None), P(), P(), P("section", None, None),
            P("section", None, None), P("section", None), P(), P(),
        ),
        out_specs=P("section", "win", None),
        check_vma=False,
    )
```

```python
import functools

import jax
import jax.numpy as jnp
from jax import lax
from jax.experimental import pallas as pl
from jax.experimental.pallas import tpu as pltpu
from jax.sharding import PartitionSpec as P

MESH = pl.DeviceIdType.MESH
TILE = 16
MB = 128
PIECES = 5
PARTS = 5


def gelu(x):
    return 0.5 * x * (1.0 + jnp.tanh(0.7978845608028654 * (x + 0.044715 * (x * x * x))))


def kernel(
    sections, slabs, height, width,
    latent, anchors, in_proj, pos_embed, w1_in, w2_in, gain_in, skip_in, out_in,
    result,
    panel, cast, marks, w1, w2, skip, proj, pos, outp, gain,
    received, skipped, produced, value, normed, units, sums, blocks, arrived,
    load_sem, mark_send, mark_recv, slab_send, slab_recv,
    next_send, next_recv, skip_send, skip_recv, done_send, done_recv, credit,
):
    section = lax.axis_index("section")
    win = lax.axis_index("win")
    last = sections - 1
    count, rows = received.shape[0], received.shape[2]
    wide = received.shape[3]
    tokens = TILE * TILE
    half = height * width
    band = half // sections
    hidden = w1.shape[1]
    model = w1.shape[0]
    piece = hidden // PIECES
    after = lax.rem(win + 1, slabs)
    before = lax.rem(win + slabs - 1, slabs)

    def load(source, target, index):
        return pltpu.make_async_copy(source, target, load_sem.at[index])

    def w1_load(p):
        return load(w1_in.at[0, pl.ds(p * (model // PIECES), model // PIECES)],
                    w1.at[pl.ds(p * (model // PIECES), model // PIECES)], p)

    def w2_load(p):
        return load(w2_in.at[0, pl.ds(p * piece, piece)], w2.at[pl.ds(p * piece, piece)], PIECES + p)

    base = 2 * PIECES
    gain_load = load(gain_in, gain, base)
    proj_load = load(in_proj, proj, base + 1)
    pos_load = load(pos_embed, pos, base + 2)

    def skip_load(part):
        return load(skip_in.at[pl.ds(part * model, model)], skip, base + 3)

    out_load = load(out_in, outp, base + 4)
    own_load = load(latent, panel.at[0], base + 5)

    barrier = pltpu.get_barrier_semaphore()

    def greet(to_section, to_win):
        pl.semaphore_signal(barrier, inc=1, device_id=(to_section, to_win), device_id_type=MESH)

    def greet_peer(step, carry):
        greet(section, lax.rem(win + step, slabs))
        return carry

    lax.fori_loop(1, slabs, greet_peer, 0)

    @pl.when(section > 0)
    def _():
        greet(section - 1, win)

    @pl.when(section == last)
    def _():
        greet(0, win)

    @pl.when(section == 0)
    def _():
        greet(1, win)

    @pl.when(section < last)
    def _():
        greet(last, win)
        greet(last, before)

    @pl.when(section == 0)
    def _():
        own_load.start()
        proj_load.start()
        pos_load.start()

    gain_load.start()
    for p in range(PIECES):
        w1_load(p).start()
    for p in range(PIECES):
        w2_load(p).start()

    @pl.when(section == 0)
    def _():
        skip_load(1).start()

    @pl.when(section == last - 1)
    def _():
        skip_load(0).start()

    @pl.when(section == last)
    def _():
        out_load.start()

    line = lax.broadcasted_iota(jnp.int32, (16, 128), 0)
    block = jnp.full((16, 128), -4096, jnp.int32)
    for i in range(anchors.shape[0]):
        block = jnp.where(line == i, anchors[i, 0], block)
        block = jnp.where(line == 8 + i, anchors[i, 1], block)
    marks[win] = block.astype(jnp.float32)

    @pl.when(section == 0)
    def _():
        pl.semaphore_wait(barrier, slabs - 1 + 2)

    @pl.when(section == 1)
    def _():
        pl.semaphore_wait(barrier, slabs - 1 + 2)

    @pl.when((section > 1) & (section < last))
    def _():
        pl.semaphore_wait(barrier, slabs - 1 + 1)

    @pl.when(section == last)
    def _():
        pl.semaphore_wait(barrier, slabs - 1 + 2 * last)

    def slab_copy():
        return pltpu.make_async_remote_copy(
            src_ref=latent, dst_ref=panel.at[1], send_sem=slab_send, recv_sem=slab_recv,
            device_id=(section, before), device_id_type=MESH)

    @pl.when(section == 0)
    def _():
        slab_copy().start()

    def mark_copy(step):
        return pltpu.make_async_remote_copy(
            src_ref=marks.at[win], dst_ref=marks.at[win],
            send_sem=mark_send.at[step], recv_sem=mark_recv.at[step],
            device_id=(section, lax.rem(win + step, slabs)), device_id_type=MESH)

    def mark_start(step, carry):
        mark_copy(step).start()
        return carry

    def mark_wait(step, carry):
        origin = lax.rem(win - step + slabs, slabs)
        pltpu.make_async_remote_copy(
            src_ref=marks.at[origin], dst_ref=marks.at[origin],
            send_sem=mark_send.at[step], recv_sem=mark_recv.at[step],
            device_id=(section, lax.rem(win + step, slabs)), device_id_type=MESH).wait_recv()
        return carry

    lax.fori_loop(1, slabs, mark_start, 0)
    lax.fori_loop(1, slabs, mark_wait, 0)

    def row_anchors(group):
        every = marks[...]
        row, col = every[:, 0:8, :], every[:, 8:16, :]
        match = col == (group * width).astype(jnp.float32)
        low = jnp.min(jnp.min(jnp.where(match, row, 4096.0), axis=0), axis=0, keepdims=True)
        high = jnp.max(jnp.max(jnp.where(match, row, -4096.0), axis=0), axis=0, keepdims=True)
        return low[:, 0:1], high[:, 0:1]

    low, high = row_anchors(win)

    def place(index, shape, dim):
        anchor = jnp.where(index < count // 2, low, high)
        inside = lax.rem(index, count // 2) * rows
        token = lax.broadcasted_iota(jnp.int32, shape, dim) + inside
        row, col = token // TILE, token % TILE
        fixed = (row * width + col % width + half * (col // width)).astype(jnp.float32)
        spot = lax.broadcasted_iota(jnp.int32, shape, 1 - dim).astype(jnp.float32)
        return (spot == fixed + anchor * float(width)).astype(jnp.bfloat16)

    def dot(a, b):
        return jnp.dot(a, b, preferred_element_type=jnp.float32)

    def joined(ref, index):
        return jnp.concatenate([ref[index, p] for p in range(PARTS)], axis=1)

    def rms_block(emit, between=None):
        v = value[...]
        factor = lax.rsqrt(jnp.mean(v * v, axis=-1, keepdims=True) + 1e-06)
        normed[...] = (v * factor * gain[...]).astype(jnp.bfloat16)
        for p in range(PIECES):
            part = gelu(dot(normed[...], w1[:, p * piece:(p + 1) * piece]))
            units[:, p * piece:(p + 1) * piece] = part.astype(jnp.bfloat16)
        if between is not None:
            between()
        for p in range(PARTS):
            here = slice(p * wide, (p + 1) * wide)
            emit(p, (value[:, here] + dot(units[...], w2[:, here])).astype(jnp.bfloat16))

    def cut(ref, index, p):
        return ref.at[index] if p is None else ref.at[index, p]

    def next_copy(index, target, p=None):
        return pltpu.make_async_remote_copy(
            src_ref=cut(produced, index, p), dst_ref=cut(received, index, p),
            send_sem=next_send.at[index], recv_sem=next_recv.at[index],
            device_id=(target, win), device_id_type=MESH)

    def skip_copy(index, p=None):
        return pltpu.make_async_remote_copy(
            src_ref=cut(skipped, index, p), dst_ref=cut(skipped, index, p),
            send_sem=skip_send.at[index], recv_sem=skip_recv.at[index],
            device_id=(last, win), device_id_type=MESH)

    def wait_first():
        gain_load.wait()
        for p in range(PIECES):
            w1_load(p).wait()

    def wait_second():
        for p in range(PIECES):
            w2_load(p).wait()

    def wait_weights():
        wait_first()
        wait_second()

    @pl.when(section == 0)
    def _():
        own_load.wait()
        proj_load.wait()
        pos_load.wait()
        slab_copy().wait_recv()
        both = jnp.concatenate([panel[0], panel[1]], axis=0)
        cast[...] = both
        wait_first()

        def step(index, carry):
            tiles = dot(place(index, (rows, 2 * half), 0), cast[...]).astype(jnp.bfloat16)
            start = pl.multiple_of(lax.rem(index, count // 2) * rows, rows)
            value[...] = dot(tiles, proj[...]) + pos[pl.ds(start, rows), :].astype(jnp.float32)

            def emit(p, part):
                produced[index, p] = part
                next_copy(index, 1, p).start()

            rms_block(emit, lambda: pl.when(index == 0)(wait_second))

            @pl.when(index == 0)
            def _():
                skip_load(1).wait()

            first = joined(produced, index)
            for p in range(PARTS):
                product = dot(first, skip[:, p * wide:(p + 1) * wide])
                skipped[index, p] = product.astype(jnp.bfloat16)

            @pl.when(index == 0)
            def _():
                for p in range(PARTS):
                    skip_copy(index, p).start()

            return carry

        lax.fori_loop(0, count, step, 0)
        for index in range(1, count):
            pl.semaphore_wait(credit, 1 if index < count - 1 else 2)
            for p in range(PARTS):
                skip_copy(index, p).start()

        def drain(index, carry):
            next_copy(index, 1).wait_send()
            skip_copy(index).wait_send()
            return carry

        lax.fori_loop(0, count, drain, 0)
        slab_copy().wait_send()

    def left(index):
        next_copy(index, section + 1).wait_send()

        @pl.when(section == 1)
        def _():
            pl.semaphore_signal(credit, inc=1, device_id=(0, win), device_id_type=MESH)

    def middle(send):
        wait_weights()

        def step(index, carry):
            next_copy(index, section + 1).wait_recv()
            value[...] = joined(received, index).astype(jnp.float32)
            send(index)

            @pl.when(index > 0)
            def _():
                left(index - 1)

            return carry

        lax.fori_loop(0, count, step, 0)
        left(count - 1)

    def send_part(index, p, part):
        produced[index, p] = part
        next_copy(index, section + 1, p).start()

    @pl.when((section > 0) & (section < last - 1))
    def _():
        middle(lambda index: rms_block(functools.partial(send_part, index)))

    @pl.when(section == last - 1)
    def _():
        def send(index):
            def emit(p, part):
                normed[:, p * wide:(p + 1) * wide] = part

            rms_block(emit)
            for p in range(PARTS):
                product = dot(normed[...], skip[:, p * wide:(p + 1) * wide])
                send_part(index, p, product.astype(jnp.bfloat16))

        skip_load(0).wait()
        middle(send)

    def done_copy(target, side):
        return pltpu.make_async_remote_copy(
            src_ref=blocks.at[pl.ds(pl.multiple_of((side * sections + target) * band, 16), band)],
            dst_ref=arrived.at[side],
            send_sem=done_send.at[side, target], recv_sem=done_recv.at[side],
            device_id=(target, after if side else win), device_id_type=MESH)

    @pl.when(section == last)
    def _():
        wait_weights()
        out_load.wait()
        sums[...] = jnp.zeros_like(sums)

        def step(index, carry):
            next_copy(index, 0).wait_recv()
            skip_copy(index).wait_recv()
            value[...] = (joined(received, index).astype(jnp.float32)
                          + joined(skipped, index).astype(jnp.float32))

            def emit(p, part):
                normed[:, p * wide:(p + 1) * wide] = part

            rms_block(emit)
            noise = dot(normed[...], outp[...]).astype(jnp.bfloat16)
            sums[...] += dot(place(index, (2 * half, rows), 1), noise)
            return carry

        lax.fori_loop(0, count, step, 0)
        blocks[...] = sums[...].astype(jnp.bfloat16)
        for target in range(sections):
            done_copy(target, 1).start()
        for target in range(sections - 1):
            done_copy(target, 0).start()
        arrived[0] = blocks[pl.ds(last * band, band), :]

    lowest, highest = row_anchors(before)
    line = lax.broadcasted_iota(jnp.int32, (band, 128), 0) // width + section * (height // sections)
    line = line.astype(jnp.float32)
    covered = jnp.zeros((band, 128), jnp.float32)
    for anchor in (low, high, lowest, highest):
        covered += jnp.where((line >= anchor) & (line < anchor + float(TILE)), 1.0, 0.0)

    @pl.when(section < last)
    def _():
        done_copy(0, 0).wait_recv()

    done_copy(0, 1).wait_recv()
    total = arrived[0].astype(jnp.float32) + arrived[1].astype(jnp.float32)
    result[...] = (total / covered[:, 0:1]).astype(jnp.bfloat16)

    @pl.when(section == last)
    def _():
        for target in range(sections):
            done_copy(target, 1).wait_send()
        for target in range(sections - 1):
            done_copy(target, 0).wait_send()

    def mark_drain(step, carry):
        mark_copy(step).wait_send()
        return carry

    lax.fori_loop(1, slabs, mark_drain, 0)


def solution(mesh):
    sections, slabs = mesh.shape["section"], mesh.shape["win"]

    def per_device(latent, anchors, in_proj, pos_embed, w1, w2, gain, skip_w, out_proj):
        height, width, feat = latent.shape
        model, hidden = w1.shape[1:]
        half = height * width
        band = half // sections
        rows = MB
        count = anchors.shape[0] * TILE * TILE // rows
        bf16, f32 = jnp.bfloat16, jnp.float32
        hbm = pl.BlockSpec(memory_space=pl.ANY)
        dma = pltpu.SemaphoreType.DMA
        out = pl.pallas_call(
            functools.partial(kernel, sections, slabs, height, width),
            out_shape=jax.ShapeDtypeStruct((band, feat), bf16),
            in_specs=[hbm, pl.BlockSpec(memory_space=pltpu.SMEM)] + [hbm] * 7,
            out_specs=pl.BlockSpec(memory_space=pltpu.VMEM),
            scratch_shapes=[
                pltpu.VMEM((2, half, feat), bf16),
                pltpu.VMEM((2 * half, feat), bf16),
                pltpu.VMEM((slabs, 16, 128), f32),
                pltpu.VMEM((model, hidden), bf16),
                pltpu.VMEM((hidden, model), bf16),
                pltpu.VMEM((model, model), bf16),
                pltpu.VMEM((feat, model), bf16),
                pltpu.VMEM((TILE * TILE, model), bf16),
                pltpu.VMEM((model, feat), bf16),
                pltpu.VMEM((1, model), f32),
                pltpu.VMEM((count, PARTS, rows, model // PARTS), bf16),
                pltpu.VMEM((count, PARTS, rows, model // PARTS), bf16),
                pltpu.VMEM((count, PARTS, rows, model // PARTS), bf16),
                pltpu.VMEM((rows, model), f32),
                pltpu.VMEM((rows, model), bf16),
                pltpu.VMEM((rows, hidden), bf16),
                pltpu.VMEM((2 * half, feat), f32),
                pltpu.VMEM((2 * half, feat), bf16),
                pltpu.VMEM((2, band, feat), bf16),
                dma((2 * PIECES + 6,)),
                dma((slabs,)),
                dma((slabs,)),
                dma,
                dma,
                dma((count,)),
                dma((count,)),
                dma((count,)),
                dma((count,)),
                dma((2, sections)),
                dma((2,)),
                pltpu.SemaphoreType.REGULAR,
            ],
            compiler_params=pltpu.CompilerParams(
                collective_id=0, has_side_effects=True, vmem_limit_bytes=56 * 1024 * 1024),
        )(latent.reshape(half, feat), anchors, in_proj, pos_embed, w1, w2, gain, skip_w, out_proj)
        return out.reshape(height // sections, width, feat)

    return jax.shard_map(
        per_device,
        mesh=mesh,
        in_specs=(
            P(None, "win", None), P("win", None), P(), P(), P("section", None, None),
            P("section", None, None), P("section", None), P(), P(),
        ),
        out_specs=P("section", "win", None),
        check_vma=False,
    )
```

```python
import functools

import jax
import jax.numpy as jnp
from jax import lax
from jax.experimental import pallas as pl
from jax.experimental.pallas import tpu as pltpu
from jax.sharding import PartitionSpec as P

MESH = pl.DeviceIdType.MESH
TILE = 16
MB = 128
PIECES = 5
PARTS = 5


def gelu(x):
    return 0.5 * x * (1.0 + jnp.tanh(0.7978845608028654 * (x + 0.044715 * (x * x * x))))


def kernel(
    sections, slabs, height, width,
    latent, anchors, in_proj, pos_embed, w1_in, w2_in, gain_in, skip_in, out_in,
    result,
    panel, cast, marks, w1, w2, skip, proj, pos, outp, gain,
    received, skipped, produced, value, normed, units, sums, blocks, arrived,
    load_sem, mark_send, mark_recv, slab_send, slab_recv,
    next_send, next_recv, skip_send, skip_recv, done_send, done_recv, credit,
):
    section = lax.axis_index("section")
    win = lax.axis_index("win")
    last = sections - 1
    count, rows = received.shape[0], received.shape[2]
    wide = received.shape[3]
    tokens = TILE * TILE
    half = height * width
    band = half // sections
    hidden = w1.shape[1]
    model = w1.shape[0]
    piece = hidden // PIECES
    after = lax.rem(win + 1, slabs)
    before = lax.rem(win + slabs - 1, slabs)

    def load(source, target, index):
        return pltpu.make_async_copy(source, target, load_sem.at[index])

    def w1_load(p):
        return load(w1_in.at[0, pl.ds(p * (model // PIECES), model // PIECES)],
                    w1.at[pl.ds(p * (model // PIECES), model // PIECES)], p)

    def w2_load(p):
        return load(w2_in.at[0, pl.ds(p * piece, piece)], w2.at[pl.ds(p * piece, piece)], PIECES + p)

    base = 2 * PIECES
    gain_load = load(gain_in, gain, base)
    proj_load = load(in_proj, proj, base + 1)
    pos_load = load(pos_embed, pos, base + 2)

    def skip_load(part):
        return load(skip_in.at[pl.ds(part * model, model)], skip, base + 3)

    out_load = load(out_in, outp, base + 4)
    own_load = load(latent, panel.at[0], base + 5)

    barrier = pltpu.get_barrier_semaphore()

    def greet(to_section, to_win):
        pl.semaphore_signal(barrier, inc=1, device_id=(to_section, to_win), device_id_type=MESH)

    def greet_peer(step, carry):
        greet(section, lax.rem(win + step, slabs))
        return carry

    lax.fori_loop(1, slabs, greet_peer, 0)

    @pl.when(section > 0)
    def _():
        greet(section - 1, win)

    @pl.when(section == last)
    def _():
        greet(0, win)

    @pl.when(section == 0)
    def _():
        greet(1, win)

    @pl.when(section < last)
    def _():
        greet(last, win)
        greet(last, before)

    @pl.when(section == 0)
    def _():
        own_load.start()
        proj_load.start()
        pos_load.start()

    gain_load.start()
    for p in range(PIECES):
        w1_load(p).start()

    line = lax.broadcasted_iota(jnp.int32, (16, 128), 0)
    block = jnp.full((16, 128), -4096, jnp.int32)
    for i in range(anchors.shape[0]):
        block = jnp.where(line == i, anchors[i, 0], block)
        block = jnp.where(line == 8 + i, anchors[i, 1], block)
    marks[win] = block.astype(jnp.float32)

    @pl.when(section == 0)
    def _():
        pl.semaphore_wait(barrier, slabs - 1 + 2)

    @pl.when(section == 1)
    def _():
        pl.semaphore_wait(barrier, slabs - 1 + 2)

    @pl.when((section > 1) & (section < last))
    def _():
        pl.semaphore_wait(barrier, slabs - 1 + 1)

    @pl.when(section == last)
    def _():
        pl.semaphore_wait(barrier, slabs - 1 + 2 * last)

    def slab_copy():
        return pltpu.make_async_remote_copy(
            src_ref=latent, dst_ref=panel.at[1], send_sem=slab_send, recv_sem=slab_recv,
            device_id=(section, before), device_id_type=MESH)

    @pl.when(section == 0)
    def _():
        slab_copy().start()

    def mark_copy(step):
        return pltpu.make_async_remote_copy(
            src_ref=marks.at[win], dst_ref=marks.at[win],
            send_sem=mark_send.at[step], recv_sem=mark_recv.at[step],
            device_id=(section, lax.rem(win + step, slabs)), device_id_type=MESH)

    def mark_start(step, carry):
        mark_copy(step).start()
        return carry

    def mark_wait(step, carry):
        origin = lax.rem(win - step + slabs, slabs)
        pltpu.make_async_remote_copy(
            src_ref=marks.at[origin], dst_ref=marks.at[origin],
            send_sem=mark_send.at[step], recv_sem=mark_recv.at[step],
            device_id=(section, lax.rem(win + step, slabs)), device_id_type=MESH).wait_recv()
        return carry

    lax.fori_loop(1, slabs, mark_start, 0)
    for p in range(PIECES):
        w2_load(p).start()

    @pl.when((section == 0) | (section == last))
    def _():
        skip_load(1).start()

    @pl.when(section == last - 1)
    def _():
        skip_load(0).start()

    @pl.when(section == last)
    def _():
        out_load.start()

    lax.fori_loop(1, slabs, mark_wait, 0)

    def row_anchors(group):
        every = marks[...]
        row, col = every[:, 0:8, :], every[:, 8:16, :]
        match = col == (group * width).astype(jnp.float32)
        low = jnp.min(jnp.min(jnp.where(match, row, 4096.0), axis=0), axis=0, keepdims=True)
        high = jnp.max(jnp.max(jnp.where(match, row, -4096.0), axis=0), axis=0, keepdims=True)
        return low[:, 0:1], high[:, 0:1]

    low, high = row_anchors(win)

    def place(index, shape, dim):
        anchor = jnp.where(index < count // 2, low, high)
        inside = lax.rem(index, count // 2) * rows
        token = lax.broadcasted_iota(jnp.int32, shape, dim) + inside
        row, col = token // TILE, token % TILE
        fixed = (row * width + col % width + half * (col // width)).astype(jnp.float32)
        spot = lax.broadcasted_iota(jnp.int32, shape, 1 - dim).astype(jnp.float32)
        return (spot == fixed + anchor * float(width)).astype(jnp.bfloat16)

    def dot(a, b):
        return jnp.dot(a, b, preferred_element_type=jnp.float32)

    def joined(ref, index):
        return jnp.concatenate([ref[index, p] for p in range(PARTS)], axis=1)

    def rms_block(emit, between=None):
        v = value[...]
        factor = lax.rsqrt(jnp.mean(v * v, axis=-1, keepdims=True) + 1e-06)
        normed[...] = (v * factor * gain[...]).astype(jnp.bfloat16)
        for p in range(PIECES):
            part = gelu(dot(normed[...], w1[:, p * piece:(p + 1) * piece]))
            units[:, p * piece:(p + 1) * piece] = part.astype(jnp.bfloat16)
        if between is not None:
            between()
        for p in range(PARTS):
            here = slice(p * wide, (p + 1) * wide)
            emit(p, (value[:, here] + dot(units[...], w2[:, here])).astype(jnp.bfloat16))

    def cut(ref, index, p):
        return ref.at[index] if p is None else ref.at[index, p]

    def next_copy(index, target, p=None):
        return pltpu.make_async_remote_copy(
            src_ref=cut(produced, index, p), dst_ref=cut(received, index, p),
            send_sem=next_send.at[index], recv_sem=next_recv.at[index],
            device_id=(target, win), device_id_type=MESH)

    def skip_copy(index, p=None):
        return pltpu.make_async_remote_copy(
            src_ref=cut(skipped, index, p), dst_ref=cut(skipped, index, p),
            send_sem=skip_send.at[index], recv_sem=skip_recv.at[index],
            device_id=(last, win), device_id_type=MESH)

    def wait_first():
        gain_load.wait()
        for p in range(PIECES):
            w1_load(p).wait()

    def wait_second():
        for p in range(PIECES):
            w2_load(p).wait()

    def wait_weights():
        wait_first()
        wait_second()

    @pl.when(section == 0)
    def _():
        own_load.wait()
        proj_load.wait()
        pos_load.wait()
        slab_copy().wait_recv()
        both = jnp.concatenate([panel[0], panel[1]], axis=0)
        cast[...] = both
        wait_first()

        def step(index, carry):
            tiles = dot(place(index, (rows, 2 * half), 0), cast[...]).astype(jnp.bfloat16)
            start = pl.multiple_of(lax.rem(index, count // 2) * rows, rows)
            value[...] = dot(tiles, proj[...]) + pos[pl.ds(start, rows), :].astype(jnp.float32)

            def emit(p, part):
                produced[index, p] = part
                next_copy(index, 1, p).start()

                @pl.when(index == 0)
                def _():
                    skipped[0, p] = part
                    skip_copy(0, p).start()

            rms_block(emit, lambda: pl.when(index == 0)(wait_second))
            return carry

        lax.fori_loop(0, count, step, 0)
        skip_load(1).wait()

        def follow(index, carry):
            first = joined(produced, index)
            for p in range(PARTS):
                product = dot(first, skip[:, p * wide:(p + 1) * wide])
                skipped[index, p] = product.astype(jnp.bfloat16)
            pl.semaphore_wait(credit, 1)

            @pl.when(index == count - 1)
            def _():
                pl.semaphore_wait(credit, 1)

            for p in range(PARTS):
                skip_copy(index, p).start()
            return carry

        lax.fori_loop(1, count, follow, 0)

        def drain(index, carry):
            next_copy(index, 1).wait_send()
            skip_copy(index).wait_send()
            return carry

        lax.fori_loop(0, count, drain, 0)
        slab_copy().wait_send()

    def left(index):
        next_copy(index, section + 1).wait_send()

        @pl.when(section == 1)
        def _():
            pl.semaphore_signal(credit, inc=1, device_id=(0, win), device_id_type=MESH)

    def middle(send):
        wait_weights()

        def step(index, carry):
            next_copy(index, section + 1).wait_recv()
            value[...] = joined(received, index).astype(jnp.float32)
            send(index)

            @pl.when(index > 0)
            def _():
                left(index - 1)

            return carry

        lax.fori_loop(0, count, step, 0)
        left(count - 1)

    def send_part(index, p, part):
        produced[index, p] = part
        next_copy(index, section + 1, p).start()

    @pl.when((section > 0) & (section < last - 1))
    def _():
        middle(lambda index: rms_block(functools.partial(send_part, index)))

    @pl.when(section == last - 1)
    def _():
        def send(index):
            def emit(p, part):
                normed[:, p * wide:(p + 1) * wide] = part

            rms_block(emit)
            for p in range(PARTS):
                product = dot(normed[...], skip[:, p * wide:(p + 1) * wide])
                send_part(index, p, product.astype(jnp.bfloat16))

        skip_load(0).wait()
        middle(send)

    def done_copy(target, side):
        return pltpu.make_async_remote_copy(
            src_ref=blocks.at[pl.ds(pl.multiple_of((side * sections + target) * band, 16), band)],
            dst_ref=arrived.at[side],
            send_sem=done_send.at[side, target], recv_sem=done_recv.at[side],
            device_id=(target, after if side else win), device_id_type=MESH)

    @pl.when(section == last)
    def _():
        wait_weights()
        out_load.wait()
        skip_load(1).wait()
        sums[...] = jnp.zeros_like(sums)

        def step(index, carry):
            next_copy(index, 0).wait_recv()
            skip_copy(index).wait_recv()
            value[...] = joined(received, index).astype(jnp.float32)

            @pl.when(index == 0)
            def _():
                value[...] += dot(joined(skipped, 0), skip[...])

            @pl.when(index > 0)
            def _():
                value[...] += joined(skipped, index).astype(jnp.float32)


            def emit(p, part):
                normed[:, p * wide:(p + 1) * wide] = part

            rms_block(emit)
            noise = dot(normed[...], outp[...]).astype(jnp.bfloat16)
            sums[...] += dot(place(index, (2 * half, rows), 1), noise)
            return carry

        lax.fori_loop(0, count, step, 0)
        blocks[...] = sums[...].astype(jnp.bfloat16)
        for target in range(sections):
            done_copy(target, 1).start()
        for target in range(sections - 1):
            done_copy(target, 0).start()
        arrived[0] = blocks[pl.ds(last * band, band), :]

    lowest, highest = row_anchors(before)
    line = lax.broadcasted_iota(jnp.int32, (band, 128), 0) // width + section * (height // sections)
    line = line.astype(jnp.float32)
    covered = jnp.zeros((band, 128), jnp.float32)
    for anchor in (low, high, lowest, highest):
        covered += jnp.where((line >= anchor) & (line < anchor + float(TILE)), 1.0, 0.0)

    @pl.when(section < last)
    def _():
        done_copy(0, 0).wait_recv()

    done_copy(0, 1).wait_recv()
    total = arrived[0].astype(jnp.float32) + arrived[1].astype(jnp.float32)
    result[...] = (total / covered[:, 0:1]).astype(jnp.bfloat16)

    @pl.when(section == last)
    def _():
        for target in range(sections):
            done_copy(target, 1).wait_send()
        for target in range(sections - 1):
            done_copy(target, 0).wait_send()

    def mark_drain(step, carry):
        mark_copy(step).wait_send()
        return carry

    lax.fori_loop(1, slabs, mark_drain, 0)


def solution(mesh):
    sections, slabs = mesh.shape["section"], mesh.shape["win"]

    def per_device(latent, anchors, in_proj, pos_embed, w1, w2, gain, skip_w, out_proj):
        height, width, feat = latent.shape
        model, hidden = w1.shape[1:]
        half = height * width
        band = half // sections
        rows = MB
        count = anchors.shape[0] * TILE * TILE // rows
        bf16, f32 = jnp.bfloat16, jnp.float32
        hbm = pl.BlockSpec(memory_space=pl.ANY)
        dma = pltpu.SemaphoreType.DMA
        out = pl.pallas_call(
            functools.partial(kernel, sections, slabs, height, width),
            out_shape=jax.ShapeDtypeStruct((band, feat), bf16),
            in_specs=[hbm, pl.BlockSpec(memory_space=pltpu.SMEM)] + [hbm] * 7,
            out_specs=pl.BlockSpec(memory_space=pltpu.VMEM),
            scratch_shapes=[
                pltpu.VMEM((2, half, feat), bf16),
                pltpu.VMEM((2 * half, feat), bf16),
                pltpu.VMEM((slabs, 16, 128), f32),
                pltpu.VMEM((model, hidden), bf16),
                pltpu.VMEM((hidden, model), bf16),
                pltpu.VMEM((model, model), bf16),
                pltpu.VMEM((feat, model), bf16),
                pltpu.VMEM((TILE * TILE, model), bf16),
                pltpu.VMEM((model, feat), bf16),
                pltpu.VMEM((1, model), f32),
                pltpu.VMEM((count, PARTS, rows, model // PARTS), bf16),
                pltpu.VMEM((count, PARTS, rows, model // PARTS), bf16),
                pltpu.VMEM((count, PARTS, rows, model // PARTS), bf16),
                pltpu.VMEM((rows, model), f32),
                pltpu.VMEM((rows, model), bf16),
                pltpu.VMEM((rows, hidden), bf16),
                pltpu.VMEM((2 * half, feat), f32),
                pltpu.VMEM((2 * half, feat), bf16),
                pltpu.VMEM((2, band, feat), bf16),
                dma((2 * PIECES + 6,)),
                dma((slabs,)),
                dma((slabs,)),
                dma,
                dma,
                dma((count,)),
                dma((count,)),
                dma((count,)),
                dma((count,)),
                dma((2, sections)),
                dma((2,)),
                pltpu.SemaphoreType.REGULAR,
            ],
            compiler_params=pltpu.CompilerParams(
                collective_id=0, has_side_effects=True, vmem_limit_bytes=56 * 1024 * 1024),
        )(latent.reshape(half, feat), anchors, in_proj, pos_embed, w1, w2, gain, skip_w, out_proj)
        return out.reshape(height // sections, width, feat)

    return jax.shard_map(
        per_device,
        mesh=mesh,
        in_specs=(
            P(None, "win", None), P("win", None), P(), P(), P("section", None, None),
            P("section", None, None), P("section", None), P(), P(),
        ),
        out_specs=P("section", "win", None),
        check_vma=False,
    )
```
